512 devices in a mesh: dp: 16 (over y, x_hi, core), segment: 2 (over x_lo), tensor: 16 (over z).
Axes of the slice: x: 4 (x_hi: 2, x_lo: 2; x = x_hi * 2 + x_lo), y: 4, z: 16, core: 2. Of those that a mesh axis runs over, the one named last changes fastest.
Arguments:
- queries: bfloat16 [16, 256, 4096], P('dp', None, ('segment', 'tensor')), may hold values from -3 to 3
- encoded: bfloat16 [16, 256, 8192], P('dp', None, ('segment', 'tensor')), may hold values from -8 to 8
- neighbour_ids: int32 [16, 8], P('dp'), may hold values from 0 to 7, each once within a row
- key_weight: bfloat16 [8192, 4096], P('dp', ('segment', 'tensor')), may hold values from -0.0625 to 0.0625
- value_weight: bfloat16 [8192, 4096], P('dp', ('segment', 'tensor')), may hold values from -0.0625 to 0.0625
- grad_context: bfloat16 [16, 256, 4096], P('dp', None, ('segment', 'tensor')), may hold values from -3 to 3
Outputs:
- context: bfloat16 [16, 256, 4096], P('dp', None, ('segment', 'tensor'))
- grad_queries: bfloat16 [16, 256, 4096], P('dp', None, ('segment', 'tensor'))
- grad_encoded: bfloat16 [16, 256, 8192], P('dp', None, ('segment', 'tensor'))
- grad_key_weight: bfloat16 [8192, 4096], P('dp', ('segment', 'tensor'))
- grad_value_weight: bfloat16 [8192, 4096], P('dp', ('segment', 'tensor'))
The draws below stay inside these ranges and needn't reach their ends.
Inputs may be any that keep to these rules, and one draw needn't show every extreme that they name: `neighbour_ids`: each row lists, at position u * 2 + j, the pool entry retrieved as neighbour j of span u; every one of the 8 entries appears exactly once in a row.
All inputs are finite; a program needn't handle non-finite values.
Results may differ from the reference program's by a relative error of at most 0.03.
Values may be sent and summed in bfloat16 or wider, within the bound.
No kernel may reach another device: no remote copies, remote signals or barrier semaphores. Data moves between devices by JAX's collectives and lax.ppermute only.
A program may use at most 64 MiB of HBM per device.

```python
import math
import jax
import jax.numpy as jnp
from jax import lax

D = 8192
HEADS = 32
HD = 128
CLEN = 64
NEIGH = 2
NTOK = 32
SPANS = 4
SEQS = 16
SEQ_TOK = 256
POOL_TOK = 256
N_SEGMENT = 2
N_TENSOR = 16


def spiked(drawn, rng, source, target, parts, factor):
    owner, partner = [(jnp.arange(drawn.shape[position]) // (drawn.shape[position] // parts)).reshape([-1 if axis == position else 1 for axis in range(drawn.ndim)]) for position in (source, target)]
    chosen = jax.random.permutation(rng, parts)[partner]
    strong = (owner == chosen) | (owner == (partner + parts // 2) % parts)
    return jnp.where(strong, factor * drawn, drawn)


def levels(rng, shape, split, low, top_value):
    loudness = 1.0
    for axis_at, parts in split:
        draws = jax.random.uniform(jax.random.fold_in(jax.random.fold_in(rng, 6), axis_at), (parts,), jnp.float32, low / len(split), top_value / len(split))
        loudness = loudness * jnp.repeat(jnp.exp(draws), shape[axis_at] // parts).reshape((-1,) + (1,) * (len(shape) - 1 - axis_at))
    return loudness


def normal_values(key, extent, deviation, limit, split=(), kind=jnp.bfloat16):
    gain = levels(key, extent, split, -0.22, 0.18) if split else 1.0
    values = jax.random.normal(key, extent, jnp.float32) * deviation * gain
    return jnp.minimum(jnp.maximum(values, -limit), limit).astype(kind)


def gaussian_with(own_key, extent, scale, limit, cuts, heavy, held_as=jnp.bfloat16):
    array = scale * jax.random.normal(own_key, extent, jnp.float32)
    if cuts:
        array = array * levels(own_key, extent, cuts, -0.22, 0.18)
    return jnp.clip(spiked(array, jax.random.fold_in(own_key, 3), *heavy), -limit, limit).astype(held_as)


def setup_inputs(seed: int = 0) -> dict:
    splits = jax.random.split(jax.random.key(seed), 7)
    return {
        "queries": normal_values(splits[0], (SEQS, SEQ_TOK, HEADS * HD), 1.0, 3.0, ((0, 16), (2, 32))),
        "encoded": gaussian_with(splits[1], (SEQS, POOL_TOK, D), 1.0, 8.0, ((0, 16), (2, 32)), (0, 2, 16, 2.0)),
        "neighbour_ids": jax.vmap(lambda own: jax.random.permutation(own, SPANS * NEIGH))(jax.random.split(splits[2], SEQS)).reshape((SEQS, SPANS * NEIGH)).astype(jnp.int32),
        "key_weight": normal_values(splits[3], (D, HEADS * HD), D ** -0.5, 0.0625, ((0, 16), (1, 32))),
        "value_weight": normal_values(splits[4], (D, HEADS * HD), D ** -0.5, 0.0625, ((0, 16), (1, 32))),
        "grad_context": normal_values(splits[5], (SEQS, SEQ_TOK, HEADS * HD), 1.0, 3.0, ((0, 16), (2, 32))),
    }


def to_blocks(row_data):
    padding = jnp.zeros((CLEN - 1,) + row_data.shape[1:], row_data.dtype)
    joined = jnp.concatenate([row_data[CLEN - 1:], padding], 0)
    return joined.reshape((SPANS, CLEN) + row_data.shape[1:])

def from_blocks(blocks):
    flattened = blocks.reshape((SPANS * CLEN,) + blocks.shape[2:])
    padding = jnp.zeros((CLEN - 1,) + flattened.shape[1:], flattened.dtype)
    return jnp.concatenate([padding, flattened[:SPANS * CLEN - (CLEN - 1)]], 0)

def reference(queries, encoded, neighbour_ids, key_weight, value_weight, grad_context):
    inverse_root = 1.0 / math.sqrt(HD)
    width = HEADS * HD
    groups = N_SEGMENT * N_TENSOR
    group_width = width // groups
    key_groups = key_weight.reshape(D, groups, group_width).transpose(1, 0, 2)
    value_groups = value_weight.reshape(D, groups, group_width).transpose(1, 0, 2)

    def one_sequence(carry, inputs):
        query_rows, enc_rows, entries, grad_rows = inputs
        keys = jnp.dot(enc_rows, key_weight, preferred_element_type=jnp.float32).astype(jnp.bfloat16)
        values = jnp.dot(enc_rows, value_weight, preferred_element_type=jnp.float32).astype(jnp.bfloat16)
        entries = entries.astype(jnp.int32)
        span_keys = jnp.take(keys.reshape(SPANS * NEIGH, NTOK, HEADS, HD), entries, axis=0)
        span_keys = span_keys.reshape(SPANS, NEIGH * NTOK, HEADS, HD)
        span_values = jnp.take(values.reshape(SPANS * NEIGH, NTOK, HEADS, HD), entries, axis=0)
        span_values = span_values.reshape(SPANS, NEIGH * NTOK, HEADS, HD)
        query_blocks = to_blocks(query_rows.reshape(SEQ_TOK, HEADS, HD))
        grad_blocks = to_blocks(grad_rows.reshape(SEQ_TOK, HEADS, HD))
        scores = jnp.einsum('uihd,ukhd->uhik', query_blocks.astype(jnp.float32), span_keys.astype(jnp.float32)) * inverse_root
        exponent = jnp.exp(scores)
        probs = exponent / lax.optimization_barrier(jnp.sum(exponent, -1, keepdims=True))
        attn_weights = probs.astype(jnp.bfloat16)
        context = jnp.einsum('uhik,ukhd->uihd', attn_weights.astype(jnp.float32), span_values.astype(jnp.float32))
        context = from_blocks(context).reshape(SEQ_TOK, width).astype(jnp.bfloat16)
        dprob = jnp.einsum('uihd,ukhd->uhik', grad_blocks.astype(jnp.float32), span_values.astype(jnp.float32))
        scaled_grad = (probs * (dprob - lax.optimization_barrier(jnp.sum(probs * dprob, -1, keepdims=True))) * inverse_root).astype(jnp.bfloat16)
        grad_query = jnp.einsum('uhik,ukhd->uihd', scaled_grad.astype(jnp.float32), span_keys.astype(jnp.float32))
        grad_query = from_blocks(grad_query).reshape(SEQ_TOK, width).astype(jnp.bfloat16)
        grad_span_keys = jnp.einsum('uhik,uihd->ukhd', scaled_grad.astype(jnp.float32), query_blocks.astype(jnp.float32)).astype(jnp.bfloat16)
        grad_span_values = jnp.einsum('uhik,uihd->ukhd', attn_weights.astype(jnp.float32), grad_blocks.astype(jnp.float32)).astype(jnp.bfloat16)
        empty = jnp.zeros((SPANS * NEIGH, NTOK, HEADS, HD), jnp.bfloat16)
        grad_keys = empty.at[entries].set(grad_span_keys.reshape(SPANS * NEIGH, NTOK, HEADS, HD)).reshape(POOL_TOK, width)
        grad_values = empty.at[entries].set(grad_span_values.reshape(SPANS * NEIGH, NTOK, HEADS, HD)).reshape(POOL_TOK, width)
        key_grad_groups = grad_keys.reshape(POOL_TOK, groups, group_width).transpose(1, 0, 2)
        value_grad_groups = grad_values.reshape(POOL_TOK, groups, group_width).transpose(1, 0, 2)

        def group_term(total, pieces):
            grad_k, grad_v, weight_k, weight_v = pieces
            term = jnp.dot(grad_k, weight_k.T, preferred_element_type=jnp.float32)
            term = term + jnp.dot(grad_v, weight_v.T, preferred_element_type=jnp.float32)
            term = lax.optimization_barrier(term.astype(jnp.bfloat16)).astype(jnp.float32)
            return (total + term, None)
        grad_enc, _ = lax.scan(group_term, jnp.zeros((POOL_TOK, D), jnp.float32), (key_grad_groups, value_grad_groups, key_groups, value_groups))
        key_part = jnp.dot(enc_rows.T, grad_keys, preferred_element_type=jnp.float32).astype(jnp.bfloat16)
        value_part = jnp.dot(enc_rows.T, grad_values, preferred_element_type=jnp.float32).astype(jnp.bfloat16)
        key_part = lax.optimization_barrier(key_part).astype(jnp.float32)
        value_part = lax.optimization_barrier(value_part).astype(jnp.float32)
        return ((carry[0] + key_part, carry[1] + value_part), (context, grad_query, grad_enc.astype(jnp.bfloat16)))
    start_sums = (jnp.zeros((D, width), jnp.float32), jnp.zeros((D, width), jnp.float32))
    sums, outputs = lax.scan(one_sequence, start_sums, (queries, encoded, neighbour_ids, grad_context))
    context, grad_queries, grad_encoded = outputs
    return (context, grad_queries, grad_encoded, sums[0].astype(jnp.bfloat16), sums[1].astype(jnp.bfloat16))
```

```python
import math

import jax
import jax.numpy as jnp
from jax import lax
from jax.experimental import pallas as pl
from jax.experimental.pallas import tpu as pltpu
from jax.sharding import Mesh, PartitionSpec as P

HD = 128
CLEN = 64
NTOK = 32
SPANS = 4
ROWS = 256
BLOCK = 256
DEPTH = 512
WIDE = 256
PIECES = 8
Z = 16
BF16 = jnp.bfloat16
F32 = jnp.float32
AXES = ("yh", "yl", "xh", "c", "s", "z")
DP = ("yh", "yl", "xh", "c")
HEADS = ("s", "z")
VMEM_LIMIT = 40 * 1024 * 1024


def dot(a, b, contract):
    return lax.dot_general(a, b, ((contract[:1], contract[1:]), ((), ())), preferred_element_type=F32)


def kernel_call(body, out_shape, n_smem, n_vmem, scratch=(), flops=0, bytes_accessed=0):
    smem = pl.BlockSpec(memory_space=pltpu.SMEM)
    vmem = pl.BlockSpec(memory_space=pltpu.VMEM)
    return pl.pallas_call(
        body,
        out_shape=out_shape,
        in_specs=[smem] * n_smem + [vmem] * n_vmem,
        out_specs=jax.tree.map(lambda _: vmem, out_shape),
        scratch_shapes=list(scratch),
        compiler_params=pltpu.CompilerParams(vmem_limit_bytes=VMEM_LIMIT),
        cost_estimate=pl.CostEstimate(
            flops=flops, bytes_accessed=bytes_accessed, transcendentals=0
        ),
    )


def project_body(me, enc, *refs):
    weights, own, other = refs[:PIECES], refs[PIECES], refs[PIECES + 1]
    total = jnp.zeros((ROWS, 2 * WIDE), F32)
    for piece in range(PIECES):
        place = jnp.bitwise_xor(me[0], piece) * 2
        for part in range(2):
            rows = weights[piece][part * BLOCK : (part + 1) * BLOCK, :]
            total = total + dot(enc[place + part], rows, (1, 0))
    own[...] = total[:, :WIDE]
    other[...] = total[:, WIDE:].astype(BF16)


def attention_body(ids, own, arrived, queries, grads, context, grad_queries, grad_kv, kv, forward, back):
    inverse_root = 1.0 / math.sqrt(HD)
    kv[...] = (own[...] + arrived[...].astype(F32)).astype(BF16)
    row = lax.broadcasted_iota(jnp.int32, (ROWS, HD), 0)

    def to_blocks(x):
        shifted = pltpu.roll(x.astype(F32), ROWS - (CLEN - 1), 0)
        return jnp.where(row < ROWS - (CLEN - 1), shifted, 0.0).astype(BF16)

    def from_blocks(x):
        return jnp.where(row >= CLEN - 1, pltpu.roll(x, CLEN - 1, 0), 0.0).astype(BF16)

    query_blocks = to_blocks(queries[...])
    grad_blocks = to_blocks(grads[...])
    for span in range(SPANS):
        starts = [pl.multiple_of(ids[0, span * 2 + j] * NTOK, NTOK) for j in range(2)]
        taken = jnp.concatenate([kv[pl.ds(start, NTOK), :] for start in starts], axis=0)
        span_keys, span_values = taken[:, :HD], taken[:, HD:]
        q = query_blocks[span * CLEN : (span + 1) * CLEN, :]
        g = grad_blocks[span * CLEN : (span + 1) * CLEN, :]
        exponent = jnp.exp(dot(q, span_keys, (1, 1)) * inverse_root)
        probs = exponent / jnp.sum(exponent, -1, keepdims=True)
        attn = probs.astype(BF16)
        dprob = dot(g, span_values, (1, 1))
        scaled = (
            probs * (dprob - jnp.sum(probs * dprob, -1, keepdims=True)) * inverse_root
        ).astype(BF16)
        forward[span * CLEN : (span + 1) * CLEN, :] = dot(attn, span_values, (1, 0))
        back[span * CLEN : (span + 1) * CLEN, :] = dot(scaled, span_keys, (1, 0))
        grad_rows = jnp.concatenate([dot(scaled, q, (0, 0)), dot(attn, g, (0, 0))], axis=1)
        grad_rows = grad_rows.astype(BF16)
        for j in range(2):
            grad_kv[pl.ds(starts[j], NTOK), :] = grad_rows[j * NTOK : (j + 1) * NTOK, :]
    context[...] = from_blocks(forward[...])
    grad_queries[...] = from_blocks(back[...])


def encoder_grad_body(me, grad_own, grad_other, *refs):
    weights, out = refs[:PIECES], refs[PIECES]
    grad = jnp.concatenate([grad_own[...], grad_other[...]], axis=1)
    for piece in range(PIECES):
        place = jnp.bitwise_xor(me[0], piece) * 2
        for part in range(2):
            rows = weights[piece][part * BLOCK : (part + 1) * BLOCK, :]
            out[place + part] = dot(grad, rows, (1, 1)).astype(BF16)


def weight_grad_body(me, enc, grad_own, grad_other, *outs):
    grad = jnp.concatenate([grad_own[...], grad_other[...]], axis=1)
    for piece in range(PIECES):
        place = jnp.bitwise_xor(me[0], piece) * 2
        for part in range(2):
            outs[piece][part * BLOCK : (part + 1) * BLOCK, :] = dot(
                enc[place + part], grad, (0, 0)
            ).astype(BF16)


def swap(x, axis):
    return lax.ppermute(x, axis, [(0, 1), (1, 0)])


def at(y, s):
    return y * 2 + s


FIRST = [(at(y, y // 2), at(3 - y, y // 2)) for y in range(4)] + [
    (at(y, 1 - y // 2), at(y, y // 2)) for y in range(4)
]
SECOND = [(at(y, 1 - y // 2), at(3 - y, y // 2)) for y in range(4)]
YS = ("yh", "yl", "s")


def reverse(pairs):
    return [(b, a) for a, b in pairs]


def diagonal(x):
    return lax.ppermute(x, ("yl", "xh"), [(i, 3 - i) for i in range(4)])


def per_device(queries, encoded, neighbour_ids, key_weight, value_weight, grad_context):
    enc = lax.all_gather(encoded[0], "z", axis=0, tiled=False)

    home = lax.axis_index("yh") == lax.axis_index("s")
    low = jnp.where(home, lax.axis_index("yl"), 1 - lax.axis_index("yl"))
    me = (low * 4 + lax.axis_index("xh") * 2 + lax.axis_index("c")).astype(jnp.int32).reshape(1)

    stacked = jnp.concatenate([key_weight, value_weight], axis=1)
    first = lax.ppermute(stacked, YS, FIRST)
    second = lax.ppermute(stacked, YS, SECOND)
    mine = jnp.concatenate(
        [jnp.where(home, stacked, first), jnp.where(home, first, second)], axis=1
    )
    gathered = [mine, swap(mine, "xh"), swap(mine, "yl"), diagonal(mine)]
    weights = []
    for piece in gathered:
        weights += [piece, swap(piece, "c")]

    half_flops = 2 * ROWS * (PIECES * DEPTH) * (2 * WIDE)
    half_bytes = 2 * (Z * ROWS * BLOCK + PIECES * DEPTH * 2 * WIDE)
    tile = jax.ShapeDtypeStruct((ROWS, WIDE), BF16)
    own, other = kernel_call(
        project_body,
        (jax.ShapeDtypeStruct((ROWS, WIDE), F32), tile),
        1,
        1 + PIECES,
        flops=half_flops,
        bytes_accessed=half_bytes,
    )(me, enc, *weights)
    arrived = swap(other, "s")

    head = jax.ShapeDtypeStruct((ROWS, HD), BF16)
    context, grad_queries, grad_own = kernel_call(
        attention_body,
        (head, head, tile),
        1,
        4,
        scratch=(
            pltpu.VMEM((ROWS, WIDE), BF16),
            pltpu.VMEM((ROWS, HD), F32),
            pltpu.VMEM((ROWS, HD), F32),
        ),
        flops=2 * ROWS * CLEN * HD * 6,
        bytes_accessed=1 << 20,
    )(neighbour_ids, own, arrived, queries[0], grad_context[0])
    grad_other = swap(grad_own, "s")

    enc_terms = kernel_call(
        encoder_grad_body,
        jax.ShapeDtypeStruct((Z, ROWS, BLOCK), BF16),
        1,
        2 + PIECES,
        flops=half_flops,
        bytes_accessed=half_bytes,
    )(me, grad_own, grad_other, *weights)
    grad_encoded = lax.psum_scatter(enc_terms, "z", scatter_dimension=0, tiled=False)

    terms = kernel_call(
        weight_grad_body,
        (jax.ShapeDtypeStruct((DEPTH, 2 * WIDE), BF16),) * PIECES,
        1,
        3,
        flops=half_flops,
        bytes_accessed=half_bytes,
    )(me, enc, grad_own, grad_other)

    def add(*parts):
        total = parts[0].astype(F32)
        for part in parts[1:]:
            total = total + part.astype(F32)
        return total.astype(BF16)

    pairs = [add(terms[2 * i], swap(terms[2 * i + 1], "c")) for i in range(4)]
    mine = add(pairs[0], swap(pairs[1], "xh"), swap(pairs[2], "yl"), diagonal(pairs[3]))
    for_same, for_other = mine[:, :WIDE], mine[:, WIDE:]
    first = lax.ppermute(jnp.where(home, for_other, for_same), YS, reverse(FIRST))
    second = lax.ppermute(for_other, YS, reverse(SECOND))
    weight_grad = add(jnp.where(home, for_same, second), first)
    return (
        context[None],
        grad_queries[None],
        grad_encoded[None],
        weight_grad[:, :HD],
        weight_grad[:, HD:],
    )


def solution(mesh):
    grid = Mesh(mesh.devices.reshape(2, 2, 2, 2, 2, Z), AXES)
    return jax.shard_map(
        per_device,
        mesh=grid,
        in_specs=(
            P(DP, None, HEADS),
            P(DP, None, HEADS),
            P(DP, None),
            P(DP, HEADS),
            P(DP, HEADS),
            P(DP, None, HEADS),
        ),
        out_specs=(
            P(DP, None, HEADS),
            P(DP, None, HEADS),
            P(DP, None, HEADS),
            P(DP, HEADS),
            P(DP, HEADS),
        ),
        check_vma=False,
    )
```

```python
import math

import jax
import jax.numpy as jnp
from jax import lax
from jax.experimental import pallas as pl
from jax.experimental.pallas import tpu as pltpu
from jax.sharding import Mesh, PartitionSpec as P

HD = 128
CLEN = 64
NTOK = 32
SPANS = 4
ROWS = 256
BLOCK = 256
WIDE = 256
PIECES = 8
GROUP = 4
BF16 = jnp.bfloat16
F32 = jnp.float32
AXES = ("yh", "yl", "xh", "c", "s", "zr", "z0")
DP = ("yh", "yl", "xh", "c")
HEADS = ("s", "zr", "z0")
SENDERS = ("yh", "yl", "xh")
VMEM_LIMIT = 40 * 1024 * 1024


def dot(a, b, contract):
    return lax.dot_general(a, b, ((contract[:1], contract[1:]), ((), ())), preferred_element_type=F32)


def kernel_call(body, out_shape, n_smem, n_vmem, scratch=(), flops=0, bytes_accessed=0):
    smem = pl.BlockSpec(memory_space=pltpu.SMEM)
    vmem = pl.BlockSpec(memory_space=pltpu.VMEM)
    return pl.pallas_call(
        body,
        out_shape=out_shape,
        in_specs=[smem] * n_smem + [vmem] * n_vmem,
        out_specs=jax.tree.map(lambda _: vmem, out_shape),
        scratch_shapes=list(scratch),
        compiler_params=pltpu.CompilerParams(vmem_limit_bytes=VMEM_LIMIT),
        cost_estimate=pl.CostEstimate(
            flops=flops, bytes_accessed=bytes_accessed, transcendentals=0
        ),
    )


def project_body(me, enc, *refs):
    weights, out = refs[:PIECES], refs[PIECES]
    for head in range(GROUP):
        columns = slice(head * WIDE, (head + 1) * WIDE)
        total = jnp.zeros((ROWS, WIDE), F32)
        for piece in range(PIECES):
            block = enc[jnp.bitwise_xor(me[0], piece)]
            total = total + dot(block, weights[piece][:, columns], (1, 0))
        out[jnp.bitwise_xor(me[1], head)] = total.astype(BF16)


def attention_body(ids, arrived, queries, grads, context, grad_queries, grad_kv, kv, forward, back):
    inverse_root = 1.0 / math.sqrt(HD)
    total = arrived[0].astype(F32)
    for part in range(1, GROUP):
        total = total + arrived[part].astype(F32)
    kv[...] = total.astype(BF16)
    row = lax.broadcasted_iota(jnp.int32, (ROWS, HD), 0)

    def to_blocks(x):
        shifted = pltpu.roll(x.astype(F32), ROWS - (CLEN - 1), 0)
        return jnp.where(row < ROWS - (CLEN - 1), shifted, 0.0).astype(BF16)

    def from_blocks(x):
        return jnp.where(row >= CLEN - 1, pltpu.roll(x, CLEN - 1, 0), 0.0).astype(BF16)

    query_blocks = to_blocks(queries[...])
    grad_blocks = to_blocks(grads[...])
    for span in range(SPANS):
        starts = [pl.multiple_of(ids[0, span * 2 + j] * NTOK, NTOK) for j in range(2)]
        taken = jnp.concatenate([kv[pl.ds(start, NTOK), :] for start in starts], axis=0)
        span_keys, span_values = taken[:, :HD], taken[:, HD:]
        q = query_blocks[span * CLEN : (span + 1) * CLEN, :]
        g = grad_blocks[span * CLEN : (span + 1) * CLEN, :]
        exponent = jnp.exp(dot(q, span_keys, (1, 1)) * inverse_root)
        probs = exponent / jnp.sum(exponent, -1, keepdims=True)
        attn = probs.astype(BF16)
        dprob = dot(g, span_values, (1, 1))
        scaled = (
            probs * (dprob - jnp.sum(probs * dprob, -1, keepdims=True)) * inverse_root
        ).astype(BF16)
        forward[span * CLEN : (span + 1) * CLEN, :] = dot(attn, span_values, (1, 0))
        back[span * CLEN : (span + 1) * CLEN, :] = dot(scaled, span_keys, (1, 0))
        grad_rows = jnp.concatenate([dot(scaled, q, (0, 0)), dot(attn, g, (0, 0))], axis=1)
        grad_rows = grad_rows.astype(BF16)
        for j in range(2):
            grad_kv[pl.ds(starts[j], NTOK), :] = grad_rows[j * NTOK : (j + 1) * NTOK, :]
    context[...] = from_blocks(forward[...])
    grad_queries[...] = from_blocks(back[...])


def heads_in_order(me, grads):
    return jnp.concatenate([grads[jnp.bitwise_xor(me[1], h)] for h in range(GROUP)], axis=1)


def encoder_grad_body(me, grads, *refs):
    weights, out = refs[:PIECES], refs[PIECES]
    grad = heads_in_order(me, grads)
    for piece in range(PIECES):
        out[jnp.bitwise_xor(me[0], piece)] = dot(grad, weights[piece][...], (1, 1)).astype(BF16)


def walk(me, near, far):
    for rest in range(4):
        for other in range(2):
            place = rest * 2 + jnp.bitwise_xor(me[2], other)
            yield place, rest, (far if other else near)


def slot(me, rest, head):
    along_s = head % 2
    sender = jnp.bitwise_xor(me[3], along_s) * 4 + (rest ^ (2 * along_s))
    return jnp.bitwise_xor(sender, me[4]) * 2 + head // 2


def weight_grad_body(me, enc, grads, near, far):
    grad = heads_in_order(me, grads)
    for place, rest, part in walk(me, near, far):
        total = dot(enc[place], grad, (0, 0)).astype(BF16)
        for head in range(GROUP):
            part[slot(me, rest, head)] = total[:, head * WIDE : (head + 1) * WIDE]


def swap(x, axis):
    return lax.ppermute(x, axis, [(0, 1), (1, 0)])


def diagonal(x):
    return lax.ppermute(x, ("yl", "xh"), [(i, 3 - i) for i in range(4)])


Y_AXES = ("yh", "yl", "s", "z0")


def exchange(home_to, other_to, flip):
    pairs = []
    for y in range(4):
        home = y // 2
        target = {"home": y, "away": 3 - y}
        for z in range(2):
            if home_to:
                pairs.append(((y, home, z), (target[home_to], home, z ^ flip)))
            if other_to:
                pairs.append(((y, 1 - home, z), (target[other_to], home, z ^ flip)))
    place = lambda at: at[0] * 4 + at[1] * 2 + at[2]
    return [(place(source), place(target)) for source, target in pairs]


EXCHANGES = [
    exchange("away", "home", 0),
    exchange(None, "away", 0),
    exchange("home", "away", 1),
    exchange("away", "home", 1),
]


def send(x, pairs):
    return lax.ppermute(x, Y_AXES, pairs)


def hop(x, by):
    return lax.ppermute(x, SENDERS, [(i, i ^ by) for i in range(8)])


def turned(flip):
    pairs = []
    for yh in range(2):
        for yl in range(2):
            for s in range(2):
                for z in range(2):
                    target = (s, yl if yh == s else 1 - yl, yh, z ^ flip)
                    pairs.append(((yh, yl, s, z), target))
    place = lambda at: ((at[0] * 2 + at[1]) * 2 + at[2]) * 2 + at[3]
    return [(place(source), place(target)) for source, target in pairs]


def turn_back(x, flip):
    pairs = [(target, source) for source, target in turned(flip)]
    return lax.ppermute(x, Y_AXES, pairs)


def per_device(queries, encoded, neighbour_ids, key_weight, value_weight, grad_context):
    enc = lax.all_gather(encoded[0], "zr", axis=0, tiled=False)

    home = lax.axis_index("yh") == lax.axis_index("s")
    low = jnp.where(home, lax.axis_index("yl"), 1 - lax.axis_index("yl"))
    block = low * 4 + lax.axis_index("xh") * 2 + lax.axis_index("c")
    own_head = lax.axis_index("z0") * 2 + lax.axis_index("s")
    places = [block, own_head, lax.axis_index("c"), lax.axis_index("s"), lax.axis_index(SENDERS)]
    me = jnp.stack(places).astype(jnp.int32)
    even = lax.axis_index("z0") == 0

    upper = jnp.concatenate([key_weight[:BLOCK], value_weight[:BLOCK]], axis=1)
    lower = jnp.concatenate([key_weight[BLOCK:], value_weight[BLOCK:]], axis=1)
    keep, give = jnp.where(even, upper, lower), jnp.where(even, lower, upper)
    got = [
        send(x, pairs) for x, pairs in zip((keep, keep, give, give), EXCHANGES, strict=True)
    ]
    mine = jnp.concatenate(
        [
            jnp.where(home, keep, got[0]),
            jnp.where(home, got[0], got[1]),
            jnp.where(home, got[2], got[3]),
            jnp.where(home, got[3], got[2]),
        ],
        axis=1,
    )
    gathered = [mine, swap(mine, "xh"), swap(mine, "yl"), diagonal(mine)]
    weights = []
    for piece in gathered:
        weights += [piece, swap(piece, "c")]

    flops = 2 * ROWS * (PIECES * BLOCK) * (GROUP * WIDE)
    moved = 2 * PIECES * BLOCK * (ROWS + GROUP * WIDE)
    group = jax.ShapeDtypeStruct((GROUP, ROWS, WIDE), BF16)
    terms = kernel_call(project_body, group, 1, 1 + PIECES, flops=flops, bytes_accessed=moved)(
        me, enc, *weights
    )
    arrived = lax.all_to_all(terms, ("z0", "s"), 0, 0, tiled=True)

    head = jax.ShapeDtypeStruct((ROWS, HD), BF16)
    context, grad_queries, grad_own = kernel_call(
        attention_body,
        (head, head, jax.ShapeDtypeStruct((ROWS, WIDE), BF16)),
        1,
        3,
        scratch=(
            pltpu.VMEM((ROWS, WIDE), BF16),
            pltpu.VMEM((ROWS, HD), F32),
            pltpu.VMEM((ROWS, HD), F32),
        ),
        flops=2 * ROWS * CLEN * HD * 6,
        bytes_accessed=1 << 20,
    )(neighbour_ids, arrived, queries[0], grad_context[0])
    grads = lax.all_gather(grad_own, ("z0", "s"), axis=0, tiled=False)

    enc_terms = kernel_call(
        encoder_grad_body,
        jax.ShapeDtypeStruct((PIECES, ROWS, BLOCK), BF16),
        1,
        1 + PIECES,
        flops=flops,
        bytes_accessed=moved,
    )(me, grads, *weights)
    grad_encoded = lax.psum_scatter(enc_terms, "zr", scatter_dimension=0, tiled=False)

    part = jax.ShapeDtypeStruct((2 * PIECES, BLOCK, WIDE), BF16)
    near, far = kernel_call(
        weight_grad_body, (part, part), 1, 2, flops=flops, bytes_accessed=moved
    )(me, enc, grads)
    near = (near.astype(F32) + swap(far, "c").astype(F32)).astype(BF16)
    near = near.reshape(8, 2, BLOCK, WIDE)
    parts = [near[0]] + [hop(near[k], k) for k in range(1, 8)]
    total = parts[0].astype(F32)
    for part in parts[1:]:
        total = total + part.astype(F32)
    total = total.astype(BF16)
    kept, given = turn_back(total[0], 0), turn_back(total[1], 1)
    upper, lower = jnp.where(even, kept, given), jnp.where(even, given, kept)
    weight_grad = jnp.concatenate([upper, lower], axis=0)
    return (
        context[None],
        grad_queries[None],
        grad_encoded[None],
        weight_grad[:, :HD],
        weight_grad[:, HD:],
    )


def solution(mesh):
    grid = Mesh(mesh.devices.reshape(2, 2, 2, 2, 2, 8, 2), AXES)
    return jax.shard_map(
        per_device,
        mesh=grid,
        in_specs=(
            P(DP, None, HEADS),
            P(DP, None, HEADS),
            P(DP, None),
            P(DP, HEADS),
            P(DP, HEADS),
            P(DP, None, HEADS),
        ),
        out_specs=(
            P(DP, None, HEADS),
            P(DP, None, HEADS),
            P(DP, None, HEADS),
            P(DP, HEADS),
            P(DP, HEADS),
        ),
        check_vma=False,
    )
```

```python
import math

import jax
import jax.numpy as jnp
from jax import lax
from jax.experimental import pallas as pl
from jax.experimental.pallas import tpu as pltpu
from jax.sharding import Mesh, PartitionSpec as P

HD = 128
CLEN = 64
NTOK = 32
SPANS = 4
ROWS = 256
BLOCK = 256
WIDE = 256
PIECES = 8
GROUP = 4
BF16 = jnp.bfloat16
F32 = jnp.float32
AXES = ("yh", "yl", "xh", "c", "s", "zr", "z0")
DP = ("yh", "yl", "xh", "c")
HEADS = ("s", "zr", "z0")
SENDERS = ("yh", "yl", "xh")
VMEM_LIMIT = 40 * 1024 * 1024


def dot(a, b, contract):
    return lax.dot_general(a, b, ((contract[:1], contract[1:]), ((), ())), preferred_element_type=F32)


def kernel_call(body, out_shape, n_smem, n_vmem, scratch=(), flops=0, bytes_accessed=0):
    smem = pl.BlockSpec(memory_space=pltpu.SMEM)
    vmem = pl.BlockSpec(memory_space=pltpu.VMEM)
    return pl.pallas_call(
        body,
        out_shape=out_shape,
        in_specs=[smem] * n_smem + [vmem] * n_vmem,
        out_specs=jax.tree.map(lambda _: vmem, out_shape),
        scratch_shapes=list(scratch),
        compiler_params=pltpu.CompilerParams(vmem_limit_bytes=VMEM_LIMIT),
        cost_estimate=pl.CostEstimate(
            flops=flops, bytes_accessed=bytes_accessed, transcendentals=0
        ),
    )


def project_body(me, enc, *refs):
    weights, out = refs[:PIECES], refs[PIECES]
    for head in range(GROUP):
        columns = slice(head * WIDE, (head + 1) * WIDE)
        total = jnp.zeros((ROWS, WIDE), F32)
        for piece in range(PIECES):
            block = enc[jnp.bitwise_xor(me[0], piece)]
            total = total + dot(block, weights[piece][:, columns], (1, 0))
        out[jnp.bitwise_xor(me[1], head)] = total.astype(BF16)


def attention_body(ids, arrived, queries, grads, context, grad_queries, grad_kv, kv, forward, back):
    inverse_root = 1.0 / math.sqrt(HD)
    total = arrived[0].astype(F32)
    for part in range(1, GROUP):
        total = total + arrived[part].astype(F32)
    kv[...] = total.astype(BF16)
    row = lax.broadcasted_iota(jnp.int32, (ROWS, HD), 0)

    def to_blocks(x):
        shifted = pltpu.roll(x.astype(F32), ROWS - (CLEN - 1), 0)
        return jnp.where(row < ROWS - (CLEN - 1), shifted, 0.0).astype(BF16)

    def from_blocks(x):
        return jnp.where(row >= CLEN - 1, pltpu.roll(x, CLEN - 1, 0), 0.0).astype(BF16)

    query_blocks = to_blocks(queries[...])
    grad_blocks = to_blocks(grads[...])
    for span in range(SPANS):
        starts = [pl.multiple_of(ids[0, span * 2 + j] * NTOK, NTOK) for j in range(2)]
        taken = jnp.concatenate([kv[pl.ds(start, NTOK), :] for start in starts], axis=0)
        span_keys, span_values = taken[:, :HD], taken[:, HD:]
        q = query_blocks[span * CLEN : (span + 1) * CLEN, :]
        g = grad_blocks[span * CLEN : (span + 1) * CLEN, :]
        exponent = jnp.exp(dot(q, span_keys, (1, 1)) * inverse_root)
        probs = exponent / jnp.sum(exponent, -1, keepdims=True)
        attn = probs.astype(BF16)
        dprob = dot(g, span_values, (1, 1))
        scaled = (
            probs * (dprob - jnp.sum(probs * dprob, -1, keepdims=True)) * inverse_root
        ).astype(BF16)
        forward[span * CLEN : (span + 1) * CLEN, :] = dot(attn, span_values, (1, 0))
        back[span * CLEN : (span + 1) * CLEN, :] = dot(scaled, span_keys, (1, 0))
        grad_rows = jnp.concatenate([dot(scaled, q, (0, 0)), dot(attn, g, (0, 0))], axis=1)
        grad_rows = grad_rows.astype(BF16)
        for j in range(2):
            grad_kv[pl.ds(starts[j], NTOK), :] = grad_rows[j * NTOK : (j + 1) * NTOK, :]
    context[...] = from_blocks(forward[...])
    grad_queries[...] = from_blocks(back[...])


def heads_in_order(me, grads):
    return jnp.concatenate([grads[jnp.bitwise_xor(me[1], h)] for h in range(GROUP)], axis=1)


def encoder_grad_body(me, grads, *refs):
    weights, out = refs[:PIECES], refs[PIECES]
    grad = heads_in_order(me, grads)
    for piece in range(PIECES):
        out[jnp.bitwise_xor(me[0], piece)] = dot(grad, weights[piece][...], (1, 1)).astype(BF16)


def walk(me, near, far):
    for rest in range(4):
        for other in range(2):
            place = rest * 2 + jnp.bitwise_xor(me[2], other)
            yield place, rest, (far if other else near)


def slot(me, rest, head):
    along_s = head % 2
    sender = jnp.bitwise_xor(me[3], along_s) * 4 + (rest ^ (2 * along_s))
    return jnp.bitwise_xor(sender, me[4]) * 2 + head // 2


def weight_grad_body(me, enc, grads, near, far):
    grad = heads_in_order(me, grads)
    for place, rest, part in walk(me, near, far):
        total = dot(enc[place], grad, (0, 0)).astype(BF16)
        for head in range(GROUP):
            part[slot(me, rest, head)] = total[:, head * WIDE : (head + 1) * WIDE]


def swap(x, axis):
    return lax.ppermute(x, axis, [(0, 1), (1, 0)])


def diagonal(x):
    return lax.ppermute(x, ("yl", "xh"), [(i, 3 - i) for i in range(4)])


Y_AXES = ("yh", "yl", "s", "z0")


def exchange(home_to, other_to, flip):
    pairs = []
    for y in range(4):
        home = y // 2
        target = {"home": y, "away": 3 - y}
        for z in range(2):
            if home_to:
                pairs.append(((y, home, z), (target[home_to], home, z ^ flip)))
            if other_to:
                pairs.append(((y, 1 - home, z), (target[other_to], home, z ^ flip)))
    place = lambda at: at[0] * 4 + at[1] * 2 + at[2]
    return [(place(source), place(target)) for source, target in pairs]


EXCHANGES = [
    exchange("away", "home", 0),
    exchange(None, "away", 0),
    exchange("home", "away", 1),
    exchange("away", "home", 1),
]


def add(*parts):
    total = parts[0].astype(F32)
    for part in parts[1:]:
        total = total + part.astype(F32)
    return total.astype(BF16)


def send(x, pairs):
    return lax.ppermute(x, Y_AXES, pairs)


def hop(x, by):
    return lax.ppermute(x, ("yh", "yl"), [(i, i ^ by) for i in range(4)])


def turned(flip):
    pairs = []
    for yh in range(2):
        for yl in range(2):
            for s in range(2):
                for z in range(2):
                    target = (s, yl if yh == s else 1 - yl, yh, z ^ flip)
                    pairs.append(((yh, yl, s, z), target))
    place = lambda at: ((at[0] * 2 + at[1]) * 2 + at[2]) * 2 + at[3]
    return [(place(source), place(target)) for source, target in pairs]


def turn_back(x, flip):
    pairs = [(target, source) for source, target in turned(flip)]
    return lax.ppermute(x, Y_AXES, pairs)


def per_device(queries, encoded, neighbour_ids, key_weight, value_weight, grad_context):
    enc = lax.all_gather(encoded[0], "zr", axis=0, tiled=False)

    home = lax.axis_index("yh") == lax.axis_index("s")
    low = jnp.where(home, lax.axis_index("yl"), 1 - lax.axis_index("yl"))
    block = low * 4 + lax.axis_index("xh") * 2 + lax.axis_index("c")
    own_head = lax.axis_index("z0") * 2 + lax.axis_index("s")
    places = [block, own_head, lax.axis_index("c"), lax.axis_index("s"), lax.axis_index(SENDERS)]
    me = jnp.stack(places).astype(jnp.int32)
    even = lax.axis_index("z0") == 0

    upper = jnp.concatenate([key_weight[:BLOCK], value_weight[:BLOCK]], axis=1)
    lower = jnp.concatenate([key_weight[BLOCK:], value_weight[BLOCK:]], axis=1)
    keep, give = jnp.where(even, upper, lower), jnp.where(even, lower, upper)
    got = [
        send(x, pairs) for x, pairs in zip((keep, keep, give, give), EXCHANGES, strict=True)
    ]
    mine = jnp.concatenate(
        [
            jnp.where(home, keep, got[0]),
            jnp.where(home, got[0], got[1]),
            jnp.where(home, got[2], got[3]),
            jnp.where(home, got[3], got[2]),
        ],
        axis=1,
    )
    gathered = [mine, swap(mine, "xh"), swap(mine, "yl"), diagonal(mine)]
    weights = []
    for piece in gathered:
        weights += [piece, swap(piece, "c")]

    flops = 2 * ROWS * (PIECES * BLOCK) * (GROUP * WIDE)
    moved = 2 * PIECES * BLOCK * (ROWS + GROUP * WIDE)
    group = jax.ShapeDtypeStruct((GROUP, ROWS, WIDE), BF16)
    terms = kernel_call(project_body, group, 1, 1 + PIECES, flops=flops, bytes_accessed=moved)(
        me, enc, *weights
    )
    arrived = lax.all_to_all(terms, ("z0", "s"), 0, 0, tiled=True)

    head = jax.ShapeDtypeStruct((ROWS, HD), BF16)
    context, grad_queries, grad_own = kernel_call(
        attention_body,
        (head, head, jax.ShapeDtypeStruct((ROWS, WIDE), BF16)),
        1,
        3,
        scratch=(
            pltpu.VMEM((ROWS, WIDE), BF16),
            pltpu.VMEM((ROWS, HD), F32),
            pltpu.VMEM((ROWS, HD), F32),
        ),
        flops=2 * ROWS * CLEN * HD * 6,
        bytes_accessed=1 << 20,
    )(neighbour_ids, arrived, queries[0], grad_context[0])
    grads = lax.all_gather(grad_own, ("z0", "s"), axis=0, tiled=False)

    enc_terms = kernel_call(
        encoder_grad_body,
        jax.ShapeDtypeStruct((PIECES, ROWS, BLOCK), BF16),
        1,
        1 + PIECES,
        flops=flops,
        bytes_accessed=moved,
    )(me, grads, *weights)
    grad_encoded = lax.psum_scatter(enc_terms, "zr", scatter_dimension=0, tiled=False)

    part = jax.ShapeDtypeStruct((2 * PIECES, BLOCK, WIDE), BF16)
    near, far = kernel_call(
        weight_grad_body, (part, part), 1, 2, flops=flops, bytes_accessed=moved
    )(me, enc, grads)
    near = (near.astype(F32) + swap(far, "c").astype(F32)).astype(BF16)
    near = near.reshape(4, 4, BLOCK, WIDE)
    near = add(near[0], hop(near[1], 1), hop(near[2], 2), hop(near[3], 3))
    total = add(near[:2], swap(near[2:], "xh"))
    kept, given = turn_back(total[0], 0), turn_back(total[1], 1)
    upper, lower = jnp.where(even, kept, given), jnp.where(even, given, kept)
    weight_grad = jnp.concatenate([upper, lower], axis=0)
    return (
        context[None],
        grad_queries[None],
        grad_encoded[None],
        weight_grad[:, :HD],
        weight_grad[:, HD:],
    )


def solution(mesh):
    grid = Mesh(mesh.devices.reshape(2, 2, 2, 2, 2, 8, 2), AXES)
    return jax.shard_map(
        per_device,
        mesh=grid,
        in_specs=(
            P(DP, None, HEADS),
            P(DP, None, HEADS),
            P(DP, None),
            P(DP, HEADS),
            P(DP, HEADS),
            P(DP, None, HEADS),
        ),
        out_specs=(
            P(DP, None, HEADS),
            P(DP, None, HEADS),
            P(DP, None, HEADS),
            P(DP, HEADS),
            P(DP, HEADS),
        ),
        check_vma=False,
    )
```

```python
import math

import jax
import jax.numpy as jnp
from jax import lax
from jax.experimental import pallas as pl
from jax.experimental.pallas import tpu as pltpu
from jax.sharding import Mesh, PartitionSpec as P

HD = 128
CLEN = 64
NTOK = 32
SPANS = 4
ROWS = 256
BLOCK = 256
WIDE = 256
PIECES = 8
GROUP = 4
BF16 = jnp.bfloat16
F32 = jnp.float32
AXES = ("yh", "yl", "xh", "c", "s", "zr", "z0")
DP = ("yh", "yl", "xh", "c")
HEADS = ("s", "zr", "z0")
SENDERS = ("yh", "yl", "xh")
VMEM_LIMIT = 40 * 1024 * 1024


def dot(a, b, contract):
    return lax.dot_general(a, b, ((contract[:1], contract[1:]), ((), ())), preferred_element_type=F32)


def kernel_call(body, out_shape, n_smem, n_vmem, scratch=(), flops=0, bytes_accessed=0):
    smem = pl.BlockSpec(memory_space=pltpu.SMEM)
    vmem = pl.BlockSpec(memory_space=pltpu.VMEM)
    return pl.pallas_call(
        body,
        out_shape=out_shape,
        in_specs=[smem] * n_smem + [vmem] * n_vmem,
        out_specs=jax.tree.map(lambda _: vmem, out_shape),
        scratch_shapes=list(scratch),
        compiler_params=pltpu.CompilerParams(vmem_limit_bytes=VMEM_LIMIT),
        cost_estimate=pl.CostEstimate(
            flops=flops, bytes_accessed=bytes_accessed, transcendentals=0
        ),
    )


def project_body(me, enc, *refs):
    weights, out = refs[:PIECES], refs[PIECES]
    for head in range(GROUP):
        columns = slice(head * WIDE, (head + 1) * WIDE)
        total = jnp.zeros((ROWS, WIDE), F32)
        for piece in range(PIECES):
            block = enc[jnp.bitwise_xor(me[0], piece)]
            total = total + dot(block, weights[piece][:, columns], (1, 0))
        out[jnp.bitwise_xor(me[1], head)] = total.astype(BF16)


def attention_body(ids, arrived, queries, grads, context, grad_queries, grad_kv, kv, forward, back):
    inverse_root = 1.0 / math.sqrt(HD)
    total = arrived[0].astype(F32)
    for part in range(1, GROUP):
        total = total + arrived[part].astype(F32)
    kv[...] = total.astype(BF16)
    row = lax.broadcasted_iota(jnp.int32, (ROWS, HD), 0)

    def to_blocks(x):
        shifted = pltpu.roll(x.astype(F32), ROWS - (CLEN - 1), 0)
        return jnp.where(row < ROWS - (CLEN - 1), shifted, 0.0).astype(BF16)

    def from_blocks(x):
        return jnp.where(row >= CLEN - 1, pltpu.roll(x, CLEN - 1, 0), 0.0).astype(BF16)

    query_blocks = to_blocks(queries[...])
    grad_blocks = to_blocks(grads[...])
    for span in range(SPANS):
        starts = [pl.multiple_of(ids[0, span * 2 + j] * NTOK, NTOK) for j in range(2)]
        taken = jnp.concatenate([kv[pl.ds(start, NTOK), :] for start in starts], axis=0)
        span_keys, span_values = taken[:, :HD], taken[:, HD:]
        q = query_blocks[span * CLEN : (span + 1) * CLEN, :]
        g = grad_blocks[span * CLEN : (span + 1) * CLEN, :]
        exponent = jnp.exp(dot(q, span_keys, (1, 1)) * inverse_root)
        probs = exponent / jnp.sum(exponent, -1, keepdims=True)
        attn = probs.astype(BF16)
        dprob = dot(g, span_values, (1, 1))
        scaled = (
            probs * (dprob - jnp.sum(probs * dprob, -1, keepdims=True)) * inverse_root
        ).astype(BF16)
        forward[span * CLEN : (span + 1) * CLEN, :] = dot(attn, span_values, (1, 0))
        back[span * CLEN : (span + 1) * CLEN, :] = dot(scaled, span_keys, (1, 0))
        grad_rows = jnp.concatenate([dot(scaled, q, (0, 0)), dot(attn, g, (0, 0))], axis=1)
        grad_rows = grad_rows.astype(BF16)
        for j in range(2):
            grad_kv[0, pl.ds(starts[j], NTOK), :] = grad_rows[j * NTOK : (j + 1) * NTOK, :]
    for copy in range(1, GROUP):
        grad_kv[copy] = grad_kv[0]
    context[...] = from_blocks(forward[...])
    grad_queries[...] = from_blocks(back[...])


def heads_in_order(me, grads):
    return jnp.concatenate([grads[jnp.bitwise_xor(me[1], h)] for h in range(GROUP)], axis=1)


def encoder_grad_body(me, grads, *refs):
    weights, out = refs[:PIECES], refs[PIECES]
    grad = heads_in_order(me, grads)
    for piece in range(PIECES):
        out[jnp.bitwise_xor(me[0], piece)] = dot(grad, weights[piece][...], (1, 1)).astype(BF16)


def walk(me, near, far):
    for rest in range(4):
        for other in range(2):
            place = rest * 2 + jnp.bitwise_xor(me[2], other)
            yield place, rest, (far if other else near)


def slot(me, rest, head):
    along_s = head % 2
    sender = jnp.bitwise_xor(me[3], along_s) * 4 + (rest ^ (2 * along_s))
    return jnp.bitwise_xor(sender, me[4]) * 2 + head // 2


def weight_grad_body(me, enc, grads, near, far):
    grad = heads_in_order(me, grads)
    for place, rest, part in walk(me, near, far):
        total = dot(enc[place], grad, (0, 0)).astype(BF16)
        for head in range(GROUP):
            part[slot(me, rest, head)] = total[:, head * WIDE : (head + 1) * WIDE]


def swap(x, axis):
    return lax.ppermute(x, axis, [(0, 1), (1, 0)])


def diagonal(x):
    return lax.ppermute(x, ("yl", "xh"), [(i, 3 - i) for i in range(4)])


Y_AXES = ("yh", "yl", "s", "z0")


def exchange(home_to, other_to, flip):
    pairs = []
    for y in range(4):
        home = y // 2
        target = {"home": y, "away": 3 - y}
        for z in range(2):
            if home_to:
                pairs.append(((y, home, z), (target[home_to], home, z ^ flip)))
            if other_to:
                pairs.append(((y, 1 - home, z), (target[other_to], home, z ^ flip)))
    place = lambda at: at[0] * 4 + at[1] * 2 + at[2]
    return [(place(source), place(target)) for source, target in pairs]


EXCHANGES = [
    exchange("away", "home", 0),
    exchange(None, "away", 0),
    exchange("home", "away", 1),
    exchange("away", "home", 1),
]


def add(*parts):
    total = parts[0].astype(F32)
    for part in parts[1:]:
        total = total + part.astype(F32)
    return total.astype(BF16)


def send(x, pairs):
    return lax.ppermute(x, Y_AXES, pairs)


def hop(x, by):
    return lax.ppermute(x, ("yh", "yl"), [(i, i ^ by) for i in range(4)])


def turned(flip):
    pairs = []
    for yh in range(2):
        for yl in range(2):
            for s in range(2):
                for z in range(2):
                    target = (s, yl if yh == s else 1 - yl, yh, z ^ flip)
                    pairs.append(((yh, yl, s, z), target))
    place = lambda at: ((at[0] * 2 + at[1]) * 2 + at[2]) * 2 + at[3]
    return [(place(source), place(target)) for source, target in pairs]


def turn_back(x, flip):
    pairs = [(target, source) for source, target in turned(flip)]
    return lax.ppermute(x, Y_AXES, pairs)


def per_device(queries, encoded, neighbour_ids, key_weight, value_weight, grad_context):
    enc = lax.all_gather(encoded[0], "zr", axis=0, tiled=False)

    home = lax.axis_index("yh") == lax.axis_index("s")
    low = jnp.where(home, lax.axis_index("yl"), 1 - lax.axis_index("yl"))
    block = low * 4 + lax.axis_index("xh") * 2 + lax.axis_index("c")
    own_head = lax.axis_index("z0") * 2 + lax.axis_index("s")
    places = [block, own_head, lax.axis_index("c"), lax.axis_index("s"), lax.axis_index(SENDERS)]
    me = jnp.stack(places).astype(jnp.int32)
    even = lax.axis_index("z0") == 0

    upper = jnp.concatenate([key_weight[:BLOCK], value_weight[:BLOCK]], axis=1)
    lower = jnp.concatenate([key_weight[BLOCK:], value_weight[BLOCK:]], axis=1)
    keep, give = jnp.where(even, upper, lower), jnp.where(even, lower, upper)
    got = [
        send(x, pairs) for x, pairs in zip((keep, keep, give, give), EXCHANGES, strict=True)
    ]
    mine = jnp.concatenate(
        [
            jnp.where(home, keep, got[0]),
            jnp.where(home, got[0], got[1]),
            jnp.where(home, got[2], got[3]),
            jnp.where(home, got[3], got[2]),
        ],
        axis=1,
    )
    gathered = [mine, swap(mine, "xh"), swap(mine, "yl"), diagonal(mine)]
    weights = []
    for piece in gathered:
        weights += [piece, swap(piece, "c")]

    flops = 2 * ROWS * (PIECES * BLOCK) * (GROUP * WIDE)
    moved = 2 * PIECES * BLOCK * (ROWS + GROUP * WIDE)
    group = jax.ShapeDtypeStruct((GROUP, ROWS, WIDE), BF16)
    terms = kernel_call(project_body, group, 1, 1 + PIECES, flops=flops, bytes_accessed=moved)(
        me, enc, *weights
    )
    arrived = lax.all_to_all(terms, ("z0", "s"), 0, 0, tiled=True)

    head = jax.ShapeDtypeStruct((ROWS, HD), BF16)
    context, grad_queries, copies = kernel_call(
        attention_body,
        (head, head, group),
        1,
        3,
        scratch=(
            pltpu.VMEM((ROWS, WIDE), BF16),
            pltpu.VMEM((ROWS, HD), F32),
            pltpu.VMEM((ROWS, HD), F32),
        ),
        flops=2 * ROWS * CLEN * HD * 6,
        bytes_accessed=1 << 20,
    )(neighbour_ids, arrived, queries[0], grad_context[0])
    grads = lax.all_to_all(copies, ("z0", "s"), 0, 0, tiled=True)

    enc_terms = kernel_call(
        encoder_grad_body,
        jax.ShapeDtypeStruct((PIECES, ROWS, BLOCK), BF16),
        1,
        1 + PIECES,
        flops=flops,
        bytes_accessed=moved,
    )(me, grads, *weights)
    grad_encoded = lax.psum_scatter(enc_terms, "zr", scatter_dimension=0, tiled=False)

    part = jax.ShapeDtypeStruct((2 * PIECES, BLOCK, WIDE), BF16)
    near, far = kernel_call(
        weight_grad_body, (part, part), 1, 2, flops=flops, bytes_accessed=moved
    )(me, enc, grads)
    near = (near.astype(F32) + swap(far, "c").astype(F32)).astype(BF16)
    near = near.reshape(4, 4, BLOCK, WIDE)
    near = add(near[0], hop(near[1], 1), hop(near[2], 2), hop(near[3], 3))
    total = add(near[:2], swap(near[2:], "xh"))
    kept, given = turn_back(total[0], 0), turn_back(total[1], 1)
    upper, lower = jnp.where(even, kept, given), jnp.where(even, given, kept)
    weight_grad = jnp.concatenate([upper, lower], axis=0)
    return (
        context[None],
        grad_queries[None],
        grad_encoded[None],
        weight_grad[:, :HD],
        weight_grad[:, HD:],
    )


def solution(mesh):
    grid = Mesh(mesh.devices.reshape(2, 2, 2, 2, 2, 8, 2), AXES)
    return jax.shard_map(
        per_device,
        mesh=grid,
        in_specs=(
            P(DP, None, HEADS),
            P(DP, None, HEADS),
            P(DP, None),
            P(DP, HEADS),
            P(DP, HEADS),
            P(DP, None, HEADS),
        ),
        out_specs=(
            P(DP, None, HEADS),
            P(DP, None, HEADS),
            P(DP, None, HEADS),
            P(DP, HEADS),
            P(DP, HEADS),
        ),
        check_vma=False,
    )
```

```python
import math

import jax
import jax.numpy as jnp
from jax import lax
from jax.experimental import pallas as pl
from jax.experimental.pallas import tpu as pltpu
from jax.sharding import Mesh, PartitionSpec as P

HD = 128
CLEN = 64
NTOK = 32
SPANS = 4
ROWS = 256
BLOCK = 256
WIDE = 256
PIECES = 8
GROUP = 4
BF16 = jnp.bfloat16
F32 = jnp.float32
AXES = ("yh", "yl", "xh", "c", "s", "zr", "z0")
DP = ("yh", "yl", "xh", "c")
HEADS = ("s", "zr", "z0")
SENDERS = ("yh", "yl", "xh")
VMEM_LIMIT = 40 * 1024 * 1024


def dot(a, b, contract):
    return lax.dot_general(a, b, ((contract[:1], contract[1:]), ((), ())), preferred_element_type=F32)


def kernel_call(body, out_shape, n_smem, n_vmem, scratch=(), flops=0, bytes_accessed=0):
    smem = pl.BlockSpec(memory_space=pltpu.SMEM)
    vmem = pl.BlockSpec(memory_space=pltpu.VMEM)
    return pl.pallas_call(
        body,
        out_shape=out_shape,
        in_specs=[smem] * n_smem + [vmem] * n_vmem,
        out_specs=jax.tree.map(lambda _: vmem, out_shape),
        scratch_shapes=list(scratch),
        compiler_params=pltpu.CompilerParams(vmem_limit_bytes=VMEM_LIMIT),
        cost_estimate=pl.CostEstimate(
            flops=flops, bytes_accessed=bytes_accessed, transcendentals=0
        ),
    )


def project_body(me, enc, *refs):
    weights, out = refs[:PIECES], refs[PIECES]
    for head in range(GROUP):
        columns = slice(head * WIDE, (head + 1) * WIDE)
        total = jnp.zeros((ROWS, WIDE), F32)
        for piece in range(PIECES):
            block = enc[jnp.bitwise_xor(me[0], piece)]
            total = total + dot(block, weights[piece][:, columns], (1, 0))
        out[jnp.bitwise_xor(me[1], head)] = total.astype(BF16)


def attention_body(ids, arrived, queries, grads, context, grad_queries, grad_kv, kv, forward, back):
    inverse_root = 1.0 / math.sqrt(HD)
    total = arrived[0].astype(F32)
    for part in range(1, GROUP):
        total = total + arrived[part].astype(F32)
    kv[...] = total.astype(BF16)
    row = lax.broadcasted_iota(jnp.int32, (ROWS, HD), 0)

    def to_blocks(x):
        shifted = pltpu.roll(x.astype(F32), ROWS - (CLEN - 1), 0)
        return jnp.where(row < ROWS - (CLEN - 1), shifted, 0.0).astype(BF16)

    def from_blocks(x):
        return jnp.where(row >= CLEN - 1, pltpu.roll(x, CLEN - 1, 0), 0.0).astype(BF16)

    query_blocks = to_blocks(queries[...])
    grad_blocks = to_blocks(grads[...])
    for span in range(SPANS):
        starts = [pl.multiple_of(ids[0, span * 2 + j] * NTOK, NTOK) for j in range(2)]
        taken = jnp.concatenate([kv[pl.ds(start, NTOK), :] for start in starts], axis=0)
        span_keys, span_values = taken[:, :HD], taken[:, HD:]
        q = query_blocks[span * CLEN : (span + 1) * CLEN, :]
        g = grad_blocks[span * CLEN : (span + 1) * CLEN, :]
        exponent = jnp.exp(dot(q, span_keys, (1, 1)) * inverse_root)
        probs = exponent / jnp.sum(exponent, -1, keepdims=True)
        attn = probs.astype(BF16)
        dprob = dot(g, span_values, (1, 1))
        scaled = (
            probs * (dprob - jnp.sum(probs * dprob, -1, keepdims=True)) * inverse_root
        ).astype(BF16)
        forward[span * CLEN : (span + 1) * CLEN, :] = dot(attn, span_values, (1, 0))
        back[span * CLEN : (span + 1) * CLEN, :] = dot(scaled, span_keys, (1, 0))
        grad_rows = jnp.concatenate([dot(scaled, q, (0, 0)), dot(attn, g, (0, 0))], axis=1)
        grad_rows = grad_rows.astype(BF16)
        for j in range(2):
            grad_kv[0, pl.ds(starts[j], NTOK), :] = grad_rows[j * NTOK : (j + 1) * NTOK, :]
    for copy in range(1, GROUP):
        grad_kv[copy] = grad_kv[0]
    context[...] = from_blocks(forward[...])
    grad_queries[...] = from_blocks(back[...])


def heads_in_order(me, grads):
    return jnp.concatenate([grads[jnp.bitwise_xor(me[1], h)] for h in range(GROUP)], axis=1)


def encoder_grad_body(me, grads, *refs):
    weights, out = refs[:PIECES], refs[PIECES]
    grad = heads_in_order(me, grads)
    for piece in range(PIECES):
        out[jnp.bitwise_xor(me[0], piece)] = dot(grad, weights[piece][...], (1, 1)).astype(BF16)


def walk(me, near, far):
    for rest in range(4):
        for other in range(2):
            place = rest * 2 + jnp.bitwise_xor(me[2], other)
            yield place, rest, (far if other else near)


def slot(me, rest, head):
    along_s = head % 2
    sender = jnp.bitwise_xor(me[3], along_s) * 4 + (rest ^ (2 * along_s))
    return jnp.bitwise_xor(sender, me[4]) * 2 + head // 2


def weight_grad_body(me, enc, grads, near, far):
    grad = heads_in_order(me, grads)
    for place, rest, part in walk(me, near, far):
        total = dot(enc[place], grad, (0, 0)).astype(BF16)
        for head in range(GROUP):
            part[slot(me, rest, head)] = total[:, head * WIDE : (head + 1) * WIDE]


def swap(x, axis):
    return lax.ppermute(x, axis, [(0, 1), (1, 0)])


def diagonal(x):
    return lax.ppermute(x, ("yl", "xh"), [(i, 3 - i) for i in range(4)])


Y_AXES = ("yh", "yl", "s", "z0")


def exchange(home_to, other_to, flip):
    pairs = []
    for y in range(4):
        home = y // 2
        target = {"home": y, "away": 3 - y}
        for z in range(2):
            if home_to:
                pairs.append(((y, home, z), (target[home_to], home, z ^ flip)))
            if other_to:
                pairs.append(((y, 1 - home, z), (target[other_to], home, z ^ flip)))
    place = lambda at: at[0] * 4 + at[1] * 2 + at[2]
    return [(place(source), place(target)) for source, target in pairs]


EXCHANGES = [
    exchange("away", "home", 0),
    exchange(None, "away", 0),
    exchange("home", "away", 1),
    exchange("away", "home", 1),
]


def add(*parts):
    total = parts[0].astype(F32)
    for part in parts[1:]:
        total = total + part.astype(F32)
    return total.astype(BF16)


def send(x, pairs):
    return lax.ppermute(x, Y_AXES, pairs)


def hop(x, by):
    return lax.ppermute(x, ("yh", "yl"), [(i, i ^ by) for i in range(4)])


def turn_back(x, across, flip):
    place = lambda at: (((at[0] * 2 + at[1]) * 2 + at[2]) * 2 + at[3]) * 2 + at[4]
    pairs = []
    for at in range(32):
        yh, yl, xh, s, z = [at >> bit & 1 for bit in (4, 3, 2, 1, 0)]
        holder = (s, yl if yh == s else 1 - yl, xh ^ across, yh, z ^ flip)
        pairs.append((place(holder), at))
    return lax.ppermute(x, ("yh", "yl", "xh", "s", "z0"), pairs)


def per_device(queries, encoded, neighbour_ids, key_weight, value_weight, grad_context):
    enc = lax.all_gather(encoded[0], "zr", axis=0, tiled=False)

    home = lax.axis_index("yh") == lax.axis_index("s")
    low = jnp.where(home, lax.axis_index("yl"), 1 - lax.axis_index("yl"))
    block = low * 4 + lax.axis_index("xh") * 2 + lax.axis_index("c")
    own_head = lax.axis_index("z0") * 2 + lax.axis_index("s")
    places = [block, own_head, lax.axis_index("c"), lax.axis_index("s"), lax.axis_index(SENDERS)]
    me = jnp.stack(places).astype(jnp.int32)
    even = lax.axis_index("z0") == 0

    upper = jnp.concatenate([key_weight[:BLOCK], value_weight[:BLOCK]], axis=1)
    lower = jnp.concatenate([key_weight[BLOCK:], value_weight[BLOCK:]], axis=1)
    keep, give = jnp.where(even, upper, lower), jnp.where(even, lower, upper)
    got = [
        send(x, pairs) for x, pairs in zip((keep, keep, give, give), EXCHANGES, strict=True)
    ]
    mine = jnp.concatenate(
        [
            jnp.where(home, keep, got[0]),
            jnp.where(home, got[0], got[1]),
            jnp.where(home, got[2], got[3]),
            jnp.where(home, got[3], got[2]),
        ],
        axis=1,
    )
    gathered = [mine, swap(mine, "xh"), swap(mine, "yl"), diagonal(mine)]
    weights = []
    for piece in gathered:
        weights += [piece, swap(piece, "c")]

    flops = 2 * ROWS * (PIECES * BLOCK) * (GROUP * WIDE)
    moved = 2 * PIECES * BLOCK * (ROWS + GROUP * WIDE)
    group = jax.ShapeDtypeStruct((GROUP, ROWS, WIDE), BF16)
    terms = kernel_call(project_body, group, 1, 1 + PIECES, flops=flops, bytes_accessed=moved)(
        me, enc, *weights
    )
    arrived = lax.all_to_all(terms, ("z0", "s"), 0, 0, tiled=True)

    head = jax.ShapeDtypeStruct((ROWS, HD), BF16)
    context, grad_queries, copies = kernel_call(
        attention_body,
        (head, head, group),
        1,
        3,
        scratch=(
            pltpu.VMEM((ROWS, WIDE), BF16),
            pltpu.VMEM((ROWS, HD), F32),
            pltpu.VMEM((ROWS, HD), F32),
        ),
        flops=2 * ROWS * CLEN * HD * 6,
        bytes_accessed=1 << 20,
    )(neighbour_ids, arrived, queries[0], grad_context[0])
    grads = lax.all_to_all(copies, ("z0", "s"), 0, 0, tiled=True)

    enc_terms = kernel_call(
        encoder_grad_body,
        jax.ShapeDtypeStruct((PIECES, ROWS, BLOCK), BF16),
        1,
        1 + PIECES,
        flops=flops,
        bytes_accessed=moved,
    )(me, grads, *weights)
    grad_encoded = lax.psum_scatter(enc_terms, "zr", scatter_dimension=0, tiled=False)

    part = jax.ShapeDtypeStruct((2 * PIECES, BLOCK, WIDE), BF16)
    near, far = kernel_call(
        weight_grad_body, (part, part), 1, 2, flops=flops, bytes_accessed=moved
    )(me, enc, grads)
    near = (near.astype(F32) + swap(far, "c").astype(F32)).astype(BF16)
    near = near.reshape(4, 4, BLOCK, WIDE)
    near = add(near[0], hop(near[1], 1), hop(near[2], 2), hop(near[3], 3))
    kept = add(turn_back(near[2], 1, 0), turn_back(near[0], 0, 0))
    given = add(turn_back(near[3], 1, 1), turn_back(near[1], 0, 1))
    upper, lower = jnp.where(even, kept, given), jnp.where(even, given, kept)
    weight_grad = jnp.concatenate([upper, lower], axis=0)
    return (
        context[None],
        grad_queries[None],
        grad_encoded[None],
        weight_grad[:, :HD],
        weight_grad[:, HD:],
    )


def solution(mesh):
    grid = Mesh(mesh.devices.reshape(2, 2, 2, 2, 2, 8, 2), AXES)
    return jax.shard_map(
        per_device,
        mesh=grid,
        in_specs=(
            P(DP, None, HEADS),
            P(DP, None, HEADS),
            P(DP, None),
            P(DP, HEADS),
            P(DP, HEADS),
            P(DP, None, HEADS),
        ),
        out_specs=(
            P(DP, None, HEADS),
            P(DP, None, HEADS),
            P(DP, None, HEADS),
            P(DP, HEADS),
            P(DP, HEADS),
        ),
        check_vma=False,
    )
```

```python
import math

import jax
import jax.numpy as jnp
from jax import lax
from jax.experimental import pallas as pl
from jax.experimental.pallas import tpu as pltpu
from jax.sharding import Mesh, PartitionSpec as P

HD = 128
CLEN = 64
NTOK = 32
SPANS = 4
ROWS = 256
BLOCK = 256
WIDE = 256
PIECES = 8
GROUP = 4
BF16 = jnp.bfloat16
F32 = jnp.float32
AXES = ("yh", "yl", "xh", "c", "s", "zr", "z0")
DP = ("yh", "yl", "xh", "c")
HEADS = ("s", "zr", "z0")
SENDERS = ("yh", "yl", "xh")
VMEM_LIMIT = 40 * 1024 * 1024


def dot(a, b, contract):
    return lax.dot_general(a, b, ((contract[:1], contract[1:]), ((), ())), preferred_element_type=F32)


def kernel_call(body, out_shape, n_smem, n_vmem, scratch=(), flops=0, bytes_accessed=0):
    smem = pl.BlockSpec(memory_space=pltpu.SMEM)
    vmem = pl.BlockSpec(memory_space=pltpu.VMEM)
    return pl.pallas_call(
        body,
        out_shape=out_shape,
        in_specs=[smem] * n_smem + [vmem] * n_vmem,
        out_specs=jax.tree.map(lambda _: vmem, out_shape),
        scratch_shapes=list(scratch),
        compiler_params=pltpu.CompilerParams(vmem_limit_bytes=VMEM_LIMIT),
        cost_estimate=pl.CostEstimate(
            flops=flops, bytes_accessed=bytes_accessed, transcendentals=0
        ),
    )


def project_body(me, enc, *refs):
    weights, out = refs[:PIECES], refs[PIECES]
    blocks = [enc[jnp.bitwise_xor(me[0], piece)] for piece in range(PIECES)]
    wide = jnp.concatenate(blocks, axis=1)
    for head in range(GROUP):
        columns = slice(head * WIDE, (head + 1) * WIDE)
        rows = jnp.concatenate([piece[:, columns] for piece in weights], axis=0)
        total = dot(wide, rows, (1, 0))
        out[jnp.bitwise_xor(me[1], head)] = total.astype(BF16)


def attention_body(ids, arrived, queries, grads, context, grad_queries, grad_kv, kv, forward, back):
    inverse_root = 1.0 / math.sqrt(HD)
    total = arrived[0].astype(F32)
    for part in range(1, GROUP):
        total = total + arrived[part].astype(F32)
    kv[...] = total.astype(BF16)
    row = lax.broadcasted_iota(jnp.int32, (ROWS, HD), 0)

    def to_blocks(x):
        shifted = pltpu.roll(x.astype(F32), ROWS - (CLEN - 1), 0)
        return jnp.where(row < ROWS - (CLEN - 1), shifted, 0.0).astype(BF16)

    def from_blocks(x):
        return jnp.where(row >= CLEN - 1, pltpu.roll(x, CLEN - 1, 0), 0.0).astype(BF16)

    query_blocks = to_blocks(queries[...])
    grad_blocks = to_blocks(grads[...])
    spans = range(SPANS)
    rows = [slice(span * CLEN, (span + 1) * CLEN) for span in spans]
    starts = [pl.multiple_of(ids[0, entry] * NTOK, NTOK) for entry in range(2 * SPANS)]
    pool = [kv[pl.ds(start, NTOK), :] for start in starts]
    taken = [jnp.concatenate(pool[2 * span : 2 * span + 2], axis=0) for span in spans]
    keys, values = [x[:, :HD] for x in taken], [x[:, HD:] for x in taken]
    qs, gs = [query_blocks[r, :] for r in rows], [grad_blocks[r, :] for r in rows]
    exponents = [jnp.exp(dot(q, k, (1, 1)) * inverse_root) for q, k in zip(qs, keys, strict=True)]
    dprobs = [dot(g, v, (1, 1)) for g, v in zip(gs, values, strict=True)]
    probs = [x / jnp.sum(x, -1, keepdims=True) for x in exponents]
    attns = [p.astype(BF16) for p in probs]
    scaled = [
        (p * (d - jnp.sum(p * d, -1, keepdims=True)) * inverse_root).astype(BF16)
        for p, d in zip(probs, dprobs, strict=True)
    ]
    for span in spans:
        forward[rows[span], :] = dot(attns[span], values[span], (1, 0))
    for span in spans:
        back[rows[span], :] = dot(scaled[span], keys[span], (1, 0))
    grad_rows = [
        jnp.concatenate([dot(sg, q, (0, 0)), dot(attn, g, (0, 0))], axis=1).astype(BF16)
        for sg, q, attn, g in zip(scaled, qs, attns, gs, strict=True)
    ]
    for entry in range(2 * SPANS):
        part = (entry % 2) * NTOK
        grad_kv[0, pl.ds(starts[entry], NTOK), :] = grad_rows[entry // 2][part : part + NTOK, :]
    for copy in range(1, GROUP):
        grad_kv[copy] = grad_kv[0]
    context[...] = from_blocks(forward[...])
    grad_queries[...] = from_blocks(back[...])


def heads_in_order(me, grads):
    return jnp.concatenate([grads[jnp.bitwise_xor(me[1], h)] for h in range(GROUP)], axis=1)


def encoder_grad_body(me, grads, *refs):
    weights, out = refs[:PIECES], refs[PIECES]
    grad = heads_in_order(me, grads)
    for piece in range(PIECES):
        out[jnp.bitwise_xor(me[0], piece)] = dot(grad, weights[piece][...], (1, 1)).astype(BF16)


def walk(me, near, far):
    for rest in range(4):
        for other in range(2):
            place = rest * 2 + jnp.bitwise_xor(me[2], other)
            yield place, rest, (far if other else near)


def slot(me, rest, head):
    along_s = head % 2
    sender = jnp.bitwise_xor(me[3], along_s) * 4 + (rest ^ (2 * along_s))
    return jnp.bitwise_xor(sender, me[4]) * 2 + head // 2


def weight_grad_body(me, enc, grads, near, far):
    grad = heads_in_order(me, grads)
    for place, rest, part in walk(me, near, far):
        total = dot(enc[place], grad, (0, 0)).astype(BF16)
        for head in range(GROUP):
            part[slot(me, rest, head)] = total[:, head * WIDE : (head + 1) * WIDE]


def swap(x, axis):
    return lax.ppermute(x, axis, [(0, 1), (1, 0)])


def diagonal(x):
    return lax.ppermute(x, ("yl", "xh"), [(i, 3 - i) for i in range(4)])


Y_AXES = ("yh", "yl", "s", "z0")


def exchange(home_to, other_to, flip):
    pairs = []
    for y in range(4):
        home = y // 2
        target = {"home": y, "away": 3 - y}
        for z in range(2):
            if home_to:
                pairs.append(((y, home, z), (target[home_to], home, z ^ flip)))
            if other_to:
                pairs.append(((y, 1 - home, z), (target[other_to], home, z ^ flip)))
    place = lambda at: at[0] * 4 + at[1] * 2 + at[2]
    return [(place(source), place(target)) for source, target in pairs]


EXCHANGES = [
    exchange("away", "home", 0),
    exchange(None, "away", 0),
    exchange("home", "away", 1),
    exchange("away", "home", 1),
]


def add(*parts):
    total = parts[0].astype(F32)
    for part in parts[1:]:
        total = total + part.astype(F32)
    return total.astype(BF16)


def send(x, pairs):
    return lax.ppermute(x, Y_AXES, pairs)


def hop(x, by):
    return lax.ppermute(x, ("yh", "yl"), [(i, i ^ by) for i in range(4)])


def turn_back(x, across, flip):
    place = lambda at: (((at[0] * 2 + at[1]) * 2 + at[2]) * 2 + at[3]) * 2 + at[4]
    pairs = []
    for at in range(32):
        yh, yl, xh, s, z = [at >> bit & 1 for bit in (4, 3, 2, 1, 0)]
        holder = (s, yl if yh == s else 1 - yl, xh ^ across, yh, z ^ flip)
        pairs.append((place(holder), at))
    return lax.ppermute(x, ("yh", "yl", "xh", "s", "z0"), pairs)


def per_device(queries, encoded, neighbour_ids, key_weight, value_weight, grad_context):
    enc = lax.all_gather(encoded[0], "zr", axis=0, tiled=False)

    home = lax.axis_index("yh") == lax.axis_index("s")
    low = jnp.where(home, lax.axis_index("yl"), 1 - lax.axis_index("yl"))
    block = low * 4 + lax.axis_index("xh") * 2 + lax.axis_index("c")
    own_head = lax.axis_index("z0") * 2 + lax.axis_index("s")
    places = [block, own_head, lax.axis_index("c"), lax.axis_index("s"), lax.axis_index(SENDERS)]
    me = jnp.stack(places).astype(jnp.int32)
    even = lax.axis_index("z0") == 0

    upper = jnp.concatenate([key_weight[:BLOCK], value_weight[:BLOCK]], axis=1)
    lower = jnp.concatenate([key_weight[BLOCK:], value_weight[BLOCK:]], axis=1)
    keep, give = jnp.where(even, upper, lower), jnp.where(even, lower, upper)
    got = [
        send(x, pairs) for x, pairs in zip((keep, keep, give, give), EXCHANGES, strict=True)
    ]
    mine = jnp.concatenate(
        [
            jnp.where(home, keep, got[0]),
            jnp.where(home, got[0], got[1]),
            jnp.where(home, got[2], got[3]),
            jnp.where(home, got[3], got[2]),
        ],
        axis=1,
    )
    gathered = [mine, swap(mine, "xh"), swap(mine, "yl"), diagonal(mine)]
    weights = []
    for piece in gathered:
        weights += [piece, swap(piece, "c")]

    flops = 2 * ROWS * (PIECES * BLOCK) * (GROUP * WIDE)
    moved = 2 * PIECES * BLOCK * (ROWS + GROUP * WIDE)
    group = jax.ShapeDtypeStruct((GROUP, ROWS, WIDE), BF16)
    terms = kernel_call(project_body, group, 1, 1 + PIECES, flops=flops, bytes_accessed=moved)(
        me, enc, *weights
    )
    arrived = lax.all_to_all(terms, ("z0", "s"), 0, 0, tiled=True)

    head = jax.ShapeDtypeStruct((ROWS, HD), BF16)
    context, grad_queries, copies = kernel_call(
        attention_body,
        (head, head, group),
        1,
        3,
        scratch=(
            pltpu.VMEM((ROWS, WIDE), BF16),
            pltpu.VMEM((ROWS, HD), F32),
            pltpu.VMEM((ROWS, HD), F32),
        ),
        flops=2 * ROWS * CLEN * HD * 6,
        bytes_accessed=1 << 20,
    )(neighbour_ids, arrived, queries[0], grad_context[0])
    grads = lax.all_to_all(copies, ("z0", "s"), 0, 0, tiled=True)

    enc_terms = kernel_call(
        encoder_grad_body,
        jax.ShapeDtypeStruct((PIECES, ROWS, BLOCK), BF16),
        1,
        1 + PIECES,
        flops=flops,
        bytes_accessed=moved,
    )(me, grads, *weights)
    grad_encoded = lax.psum_scatter(enc_terms, "zr", scatter_dimension=0, tiled=False)

    part = jax.ShapeDtypeStruct((2 * PIECES, BLOCK, WIDE), BF16)
    near, far = kernel_call(
        weight_grad_body, (part, part), 1, 2, flops=flops, bytes_accessed=moved
    )(me, enc, grads)
    near = (near.astype(F32) + swap(far, "c").astype(F32)).astype(BF16)
    near = near.reshape(4, 4, BLOCK, WIDE)
    near = add(near[0], hop(near[1], 1), hop(near[2], 2), hop(near[3], 3))
    kept = add(turn_back(near[2], 1, 0), turn_back(near[0], 0, 0))
    given = add(turn_back(near[3], 1, 1), turn_back(near[1], 0, 1))
    upper, lower = jnp.where(even, kept, given), jnp.where(even, given, kept)
    weight_grad = jnp.concatenate([upper, lower], axis=0)
    return (
        context[None],
        grad_queries[None],
        grad_encoded[None],
        weight_grad[:, :HD],
        weight_grad[:, HD:],
    )


def solution(mesh):
    grid = Mesh(mesh.devices.reshape(2, 2, 2, 2, 2, 8, 2), AXES)
    return jax.shard_map(
        per_device,
        mesh=grid,
        in_specs=(
            P(DP, None, HEADS),
            P(DP, None, HEADS),
            P(DP, None),
            P(DP, HEADS),
            P(DP, HEADS),
            P(DP, None, HEADS),
        ),
        out_specs=(
            P(DP, None, HEADS),
            P(DP, None, HEADS),
            P(DP, None, HEADS),
            P(DP, HEADS),
            P(DP, HEADS),
        ),
        check_vma=False,
    )
```

```python
import math

import jax
import jax.numpy as jnp
from jax import lax
from jax.experimental import pallas as pl
from jax.experimental.pallas import tpu as pltpu
from jax.sharding import Mesh, PartitionSpec as P

HD = 128
CLEN = 64
NTOK = 32
SPANS = 4
ROWS = 256
BLOCK = 256
WIDE = 256
PIECES = 8
GROUP = 4
BF16 = jnp.bfloat16
F32 = jnp.float32
AXES = ("yh", "yl", "xh", "c", "s", "zr", "z0")
DP = ("yh", "yl", "xh", "c")
HEADS = ("s", "zr", "z0")
SENDERS = ("yh", "yl", "xh")
VMEM_LIMIT = 40 * 1024 * 1024


def dot(a, b, contract):
    return lax.dot_general(a, b, ((contract[:1], contract[1:]), ((), ())), preferred_element_type=F32)


def kernel_call(body, out_shape, n_smem, n_vmem, scratch=(), flops=0, bytes_accessed=0):
    smem = pl.BlockSpec(memory_space=pltpu.SMEM)
    vmem = pl.BlockSpec(memory_space=pltpu.VMEM)
    return pl.pallas_call(
        body,
        out_shape=out_shape,
        in_specs=[smem] * n_smem + [vmem] * n_vmem,
        out_specs=jax.tree.map(lambda _: vmem, out_shape),
        scratch_shapes=list(scratch),
        compiler_params=pltpu.CompilerParams(vmem_limit_bytes=VMEM_LIMIT),
        cost_estimate=pl.CostEstimate(
            flops=flops, bytes_accessed=bytes_accessed, transcendentals=0
        ),
    )


def project_body(me, enc, *refs):
    weights, out = refs[:PIECES], refs[PIECES]
    blocks = [enc[jnp.bitwise_xor(me[0], piece)] for piece in range(PIECES)]
    wide = jnp.concatenate(blocks, axis=1)
    for head in range(GROUP):
        columns = slice(head * WIDE, (head + 1) * WIDE)
        rows = jnp.concatenate([piece[:, columns] for piece in weights], axis=0)
        total = dot(wide, rows, (1, 0))
        out[jnp.bitwise_xor(me[1], head)] = total.astype(BF16)


def attention_body(ids, arrived, queries, grads, context, grad_queries, grad_kv, kv, forward, back):
    inverse_root = 1.0 / math.sqrt(HD)
    total = arrived[0].astype(F32)
    for part in range(1, GROUP):
        total = total + arrived[part].astype(F32)
    kv[...] = total.astype(BF16)
    row = lax.broadcasted_iota(jnp.int32, (ROWS, HD), 0)

    def to_blocks(x):
        shifted = pltpu.roll(x.astype(F32), ROWS - (CLEN - 1), 0)
        return jnp.where(row < ROWS - (CLEN - 1), shifted, 0.0).astype(BF16)

    def from_blocks(x):
        return jnp.where(row >= CLEN - 1, pltpu.roll(x, CLEN - 1, 0), 0.0).astype(BF16)

    query_blocks = to_blocks(queries[...])
    grad_blocks = to_blocks(grads[...])
    spans = range(SPANS)
    rows = [slice(span * CLEN, (span + 1) * CLEN) for span in spans]
    starts = [pl.multiple_of(ids[0, entry] * NTOK, NTOK) for entry in range(2 * SPANS)]
    pool = [kv[pl.ds(start, NTOK), :] for start in starts]
    taken = [jnp.concatenate(pool[2 * span : 2 * span + 2], axis=0) for span in spans]
    keys, values = [x[:, :HD] for x in taken], [x[:, HD:] for x in taken]
    qs, gs = [query_blocks[r, :] for r in rows], [grad_blocks[r, :] for r in rows]
    exponents = [jnp.exp(dot(q, k, (1, 1)) * inverse_root) for q, k in zip(qs, keys, strict=True)]
    dprobs = [dot(g, v, (1, 1)) for g, v in zip(gs, values, strict=True)]
    probs = [x / jnp.sum(x, -1, keepdims=True) for x in exponents]
    attns = [p.astype(BF16) for p in probs]
    scaled = [
        (p * (d - jnp.sum(p * d, -1, keepdims=True)) * inverse_root).astype(BF16)
        for p, d in zip(probs, dprobs, strict=True)
    ]
    for span in spans:
        forward[rows[span], :] = dot(attns[span], values[span], (1, 0))
    for span in spans:
        back[rows[span], :] = dot(scaled[span], keys[span], (1, 0))
    grad_rows = [
        jnp.concatenate([dot(sg, q, (0, 0)), dot(attn, g, (0, 0))], axis=1).astype(BF16)
        for sg, q, attn, g in zip(scaled, qs, attns, gs, strict=True)
    ]
    for entry in range(2 * SPANS):
        part = (entry % 2) * NTOK
        grad_kv[0, pl.ds(starts[entry], NTOK), :] = grad_rows[entry // 2][part : part + NTOK, :]
    for copy in range(1, GROUP):
        grad_kv[copy] = grad_kv[0]
    context[...] = from_blocks(forward[...])
    grad_queries[...] = from_blocks(back[...])


def heads_in_order(me, grads):
    return jnp.concatenate([grads[jnp.bitwise_xor(me[1], h)] for h in range(GROUP)], axis=1)


def encoder_grad_body(me, grads, *refs):
    weights, out = refs[:PIECES], refs[PIECES]
    grad = heads_in_order(me, grads)
    for piece in range(PIECES):
        out[jnp.bitwise_xor(me[0], piece)] = dot(grad, weights[piece][...], (1, 1)).astype(BF16)


def walk(me, near, far):
    for rest in range(4):
        for other in range(2):
            place = rest * 2 + jnp.bitwise_xor(me[2], other)
            yield place, rest, (far if other else near)


def slot(me, rest, head):
    along_s = head % 2
    sender = jnp.bitwise_xor(me[3], along_s) * 4 + (rest ^ (2 * along_s))
    return jnp.bitwise_xor(sender, me[4]) * 2 + head // 2


def weight_grad_body(me, enc, grads, near, far):
    grad = heads_in_order(me, grads)
    for place, rest, part in walk(me, near, far):
        total = dot(enc[place], grad, (0, 0)).astype(BF16)
        for head in range(GROUP):
            part[slot(me, rest, head)] = total[:, head * WIDE : (head + 1) * WIDE]


def swap(x, axis):
    return lax.ppermute(x, axis, [(0, 1), (1, 0)])


def diagonal(x):
    return lax.ppermute(x, ("yl", "xh"), [(i, 3 - i) for i in range(4)])


Y_AXES = ("yh", "yl", "s", "z0")


def exchange(home_to, other_to, flip):
    pairs = []
    for y in range(4):
        home = y // 2
        target = {"home": y, "away": 3 - y}
        for z in range(2):
            if home_to:
                pairs.append(((y, home, z), (target[home_to], home, z ^ flip)))
            if other_to:
                pairs.append(((y, 1 - home, z), (target[other_to], home, z ^ flip)))
    place = lambda at: at[0] * 4 + at[1] * 2 + at[2]
    return [(place(source), place(target)) for source, target in pairs]


EXCHANGES = [
    exchange("away", "home", 0),
    exchange(None, "away", 0),
    exchange("home", "away", 1),
    exchange("away", "home", 1),
]


def add(*parts):
    total = parts[0].astype(F32)
    for part in parts[1:]:
        total = total + part.astype(F32)
    return total.astype(BF16)


def send(x, pairs):
    return lax.ppermute(x, Y_AXES, pairs)


def hop(x, by):
    return lax.ppermute(x, ("yh", "yl"), [(i, i ^ by) for i in range(4)])


def turn_back(x, across, flip):
    place = lambda at: (((at[0] * 2 + at[1]) * 2 + at[2]) * 2 + at[3]) * 2 + at[4]
    pairs = []
    for at in range(32):
        yh, yl, xh, s, z = [at >> bit & 1 for bit in (4, 3, 2, 1, 0)]
        holder = (s, yl if yh == s else 1 - yl, xh ^ across, yh, z ^ flip)
        pairs.append((place(holder), at))
    return lax.ppermute(x, ("yh", "yl", "xh", "s", "z0"), pairs)


def per_device(queries, encoded, neighbour_ids, key_weight, value_weight, grad_context):
    enc = lax.all_gather(encoded[0], "zr", axis=0, tiled=False)

    home = lax.axis_index("yh") == lax.axis_index("s")
    low = jnp.where(home, lax.axis_index("yl"), 1 - lax.axis_index("yl"))
    block = low * 4 + lax.axis_index("xh") * 2 + lax.axis_index("c")
    own_head = lax.axis_index("z0") * 2 + lax.axis_index("s")
    places = [block, own_head, lax.axis_index("c"), lax.axis_index("s"), lax.axis_index(SENDERS)]
    me = jnp.stack(places).astype(jnp.int32)
    even = lax.axis_index("z0") == 0

    upper = jnp.concatenate([key_weight[:BLOCK], value_weight[:BLOCK]], axis=1)
    lower = jnp.concatenate([key_weight[BLOCK:], value_weight[BLOCK:]], axis=1)
    keep, give = jnp.where(even, upper, lower), jnp.where(even, lower, upper)
    got = [
        send(x, pairs) for x, pairs in zip((keep, keep, give, give), EXCHANGES, strict=True)
    ]
    mine = jnp.concatenate(
        [
            jnp.where(home, keep, got[0]),
            jnp.where(home, got[0], got[1]),
            jnp.where(home, got[2], got[3]),
            jnp.where(home, got[3], got[2]),
        ],
        axis=1,
    )
    gathered = [mine, swap(mine, "xh"), swap(mine, "yl"), diagonal(mine)]
    weights = []
    for piece in gathered:
        weights += [piece, swap(piece, "c")]

    flops = 2 * ROWS * (PIECES * BLOCK) * (GROUP * WIDE)
    moved = 2 * PIECES * BLOCK * (ROWS + GROUP * WIDE)
    group = jax.ShapeDtypeStruct((GROUP, ROWS, WIDE), BF16)
    terms = kernel_call(project_body, group, 1, 1 + PIECES, flops=flops, bytes_accessed=moved)(
        me, enc, *weights
    )
    arrived = lax.all_to_all(terms, ("z0", "s"), 0, 0, tiled=True)

    head = jax.ShapeDtypeStruct((ROWS, HD), BF16)
    context, grad_queries, copies = kernel_call(
        attention_body,
        (head, head, group),
        1,
        3,
        scratch=(
            pltpu.VMEM((ROWS, WIDE), BF16),
            pltpu.VMEM((ROWS, HD), F32),
            pltpu.VMEM((ROWS, HD), F32),
        ),
        flops=2 * ROWS * CLEN * HD * 6,
        bytes_accessed=1 << 20,
    )(neighbour_ids, arrived, queries[0], grad_context[0])
    grads = lax.all_to_all(copies, ("z0", "s"), 0, 0, tiled=True)

    enc_terms = kernel_call(
        encoder_grad_body,
        jax.ShapeDtypeStruct((PIECES, ROWS, BLOCK), BF16),
        1,
        1 + PIECES,
        flops=flops,
        bytes_accessed=moved,
    )(me, grads, *weights)
    grad_encoded = lax.psum_scatter(enc_terms, "zr", scatter_dimension=0, tiled=False)

    part = jax.ShapeDtypeStruct((2 * PIECES, BLOCK, WIDE), BF16)
    near, far = kernel_call(
        weight_grad_body, (part, part), 1, 2, flops=flops, bytes_accessed=moved
    )(me, enc, grads)
    near = (near.astype(F32) + swap(far, "c").astype(F32)).astype(BF16)
    near = near.reshape(4, 4, BLOCK, WIDE)
    near = add(near[0], hop(near[2], 2), hop(near[1], 1), hop(near[3], 3))
    kept = add(turn_back(near[2], 1, 0), turn_back(near[0], 0, 0))
    given = add(turn_back(near[3], 1, 1), turn_back(near[1], 0, 1))
    upper, lower = jnp.where(even, kept, given), jnp.where(even, given, kept)
    weight_grad = jnp.concatenate([upper, lower], axis=0)
    return (
        context[None],
        grad_queries[None],
        grad_encoded[None],
        weight_grad[:, :HD],
        weight_grad[:, HD:],
    )


def solution(mesh):
    grid = Mesh(mesh.devices.reshape(2, 2, 2, 2, 2, 8, 2), AXES)
    return jax.shard_map(
        per_device,
        mesh=grid,
        in_specs=(
            P(DP, None, HEADS),
            P(DP, None, HEADS),
            P(DP, None),
            P(DP, HEADS),
            P(DP, HEADS),
            P(DP, None, HEADS),
        ),
        out_specs=(
            P(DP, None, HEADS),
            P(DP, None, HEADS),
            P(DP, None, HEADS),
            P(DP, HEADS),
            P(DP, HEADS),
        ),
        check_vma=False,
    )
```
